128 devices in a mesh: row: 32 (over z, x, core), col: 4 (over y).
Axes of the slice: x: 4, y: 4, z: 4, core: 2. Of those that a mesh axis runs over, the one named last changes fastest.
Arguments:
- blocks: bfloat16 [65536, 128, 128], P(('row', 'col')), may hold values from -0.046875 to 0.046875
- block_row: int32 [65536], P(('row', 'col')), may hold values from -1 to 7, as said below
- block_col: int32 [65536], P(('row', 'col')), may hold values from -1 to 31, as said below
- sketch: bfloat16 [524288, 128], P(('row', 'col')), may hold values from -6 to 6
Outputs:
- basis: float32 [32768, 128], P(('row', 'col'))
- factor: float32 [128, 128], replicated
The draws below stay inside these ranges and needn't reach their ends.
Inputs may be any that keep to these rules, and one draw needn't show every extreme that they name: The 512 slots of one device form 32 groups of 16 consecutive slots; in each group the live slots come first, 1 to 16 of them, then padding marked -1 in block_row and block_col alike; in every draw some group of some device is full. `block_col`: no two live slots of one group of one device name the same pair of block row and block column offset.
All inputs are finite; a program needn't handle non-finite values.
Results may differ from the reference program's by a relative error of at most 0.0003.
Values may be sent and summed in bfloat16 or wider, within the bound.
A program may use at most 192 MiB of HBM per device.

```python
import jax
import jax.numpy as jnp
from jax import lax

BLK = 128
RANK = 128
BR_DEV = 8
XB_DEV = 32
CAP = 16
SLOTS_ALL = 65536
NMAT = 524288
N_ROW = 32
N_COL = 4


def pattern(key):
    device_total = N_ROW * N_COL
    key_count, key_perm = jax.random.split(key)
    counts = jax.random.randint(key_count, (device_total, N_ROW), 1, CAP + 1)
    row_index = jnp.arange(device_total, dtype=jnp.int32) // N_COL
    col_index = jnp.arange(device_total, dtype=jnp.int32) % N_COL
    diagonal_hit = (row_index[:, None] == jnp.arange(N_ROW, dtype=jnp.int32)[None, :]) & (col_index[:, None] == 0)
    counts = jnp.where(diagonal_hit, CAP, counts).reshape(-1)
    perm_keys = jax.random.split(key_perm, device_total * N_ROW)
    shuffled = jax.vmap(lambda single: jax.random.permutation(single, BR_DEV * XB_DEV)[:CAP])(perm_keys)
    is_live = jnp.arange(CAP, dtype=jnp.int32)[None, :] < counts[:, None]
    row_ids = jnp.where(is_live, shuffled // XB_DEV, -1).reshape(-1).astype(jnp.int32)
    col_ids = jnp.where(is_live, shuffled % XB_DEV, -1).reshape(-1).astype(jnp.int32)
    return (row_ids, col_ids)


def draw_block_row(key, part):
    row_ids, col_ids = pattern(key)
    return row_ids


def draw_block_col(key, part):
    row_ids, col_ids = pattern(key)
    return col_ids


def levels(key, dims, cuts, smallest, top_value):
    def one(dim, shards_of):
        heights = jax.random.uniform(jax.random.fold_in(jax.random.fold_in(key, 6), dim), (shards_of,), jnp.float32, smallest / len(cuts), top_value / len(cuts))
        return jnp.repeat(jnp.exp(heights), dims[dim] // shards_of).reshape((-1,) + (1,) * (len(dims) - dim - 1))

    factor_of = one(*cuts[0])
    for cut in cuts[1:]:
        factor_of = factor_of * one(*cut)
    return factor_of


def bell_draw(rng, dims, scale, limit, shards=(), kind=jnp.bfloat16):
    gain = levels(rng, dims, shards, -0.22, 0.18) if shards else 1.0
    array = jax.random.normal(rng, dims, jnp.float32) * scale * gain
    return jnp.minimum(jnp.maximum(array, -limit), limit).astype(kind)


def setup_inputs(seed: int = 0) -> dict:
    seeds = jax.random.split(jax.random.key(seed), 5)
    blocks = bell_draw(seeds[0], (SLOTS_ALL, BLK, BLK), (BLK * N_ROW * N_COL) ** -0.5, 0.046875, ((0, 128),))
    block_row = draw_block_row(jax.random.fold_in(seeds[4], 71), 0)
    block_col = draw_block_col(jax.random.fold_in(seeds[4], 71), 0)
    sketch = bell_draw(seeds[3], (NMAT, RANK), 1.0, 6.0, ((0, 128),))
    return dict(blocks=blocks, block_row=block_row, block_col=block_col, sketch=sketch)


def upper_factor(gram):
    order = gram.shape[0]
    columns = jnp.arange(order, dtype=jnp.int32)

    def one_row(index, upper):
        column = lax.dynamic_slice_in_dim(upper, index, 1, 1)[:, 0]
        gram_row = lax.dynamic_slice_in_dim(gram, index, 1, 0)[0]
        remain = gram_row - jnp.dot(column, upper, precision=lax.Precision.HIGHEST)
        pivot = lax.dynamic_slice_in_dim(remain, index, 1, 0)[0]
        new_row = jnp.where(columns >= index, remain / jnp.sqrt(pivot), jnp.zeros_like(remain))
        return lax.dynamic_update_slice_in_dim(upper, new_row[None, :], index, 0)
    return lax.fori_loop(0, order, one_row, jnp.zeros_like(gram))

def upper_inverse(upper):
    order = upper.shape[0]
    columns = jnp.arange(order, dtype=jnp.int32)

    def one_row(turn, inverse):
        index = order - 1 - turn
        upper_row = lax.dynamic_slice_in_dim(upper, index, 1, 0)[0]
        unit = (columns == index).astype(upper.dtype)
        remain = unit - jnp.dot(upper_row, inverse, precision=lax.Precision.HIGHEST)
        pivot = lax.dynamic_slice_in_dim(upper_row, index, 1, 0)[0]
        return lax.dynamic_update_slice_in_dim(inverse, (remain / pivot)[None, :], index, 0)
    return lax.fori_loop(0, order, one_row, jnp.zeros_like(upper))

def reference(blocks, block_row, block_col, sketch):
    device_total = N_ROW * N_COL
    grouped = blocks.reshape(device_total, N_ROW, CAP, BLK, BLK)
    row_ids = block_row.reshape(device_total, N_ROW, CAP)
    col_ids = block_col.reshape(device_total, N_ROW, CAP)
    sketch_blocks = sketch.reshape(device_total * XB_DEV, BLK, RANK)

    def device_part(device):
        column = device % N_COL
        owners = jnp.arange(N_ROW, dtype=jnp.int32)[:, None] * N_COL + column
        position = owners * XB_DEV + jnp.clip(col_ids[device], 0, XB_DEV - 1)
        chosen = sketch_blocks[position]
        products = jnp.einsum('tkab,tkbc->tkac', grouped[device].astype(jnp.float32), chosen.astype(jnp.float32), precision=lax.Precision.HIGHEST)
        selector = (row_ids[device][None, :, :] == jnp.arange(BR_DEV, dtype=jnp.int32)[:, None, None]).astype(jnp.float32)
        return jnp.einsum('btk,tkac->bac', selector, products, precision=lax.Precision.HIGHEST)
    pieces = lax.map(device_part, jnp.arange(device_total, dtype=jnp.int32))
    sampled = lax.optimization_barrier(jnp.sum(pieces.reshape(N_ROW, N_COL, BR_DEV * BLK, RANK), axis=1)).reshape(N_ROW * BR_DEV * BLK, RANK)
    gram_matrix = jnp.dot(sampled.T, sampled, precision=lax.Precision.HIGHEST)
    factor = upper_factor(gram_matrix)
    basis = jnp.dot(sampled, upper_inverse(factor), precision=lax.Precision.HIGHEST)
    return (basis, factor)
```

```python
import functools

import jax
import jax.numpy as jnp
from jax import lax
from jax.experimental import pallas as pl
from jax.experimental.pallas import tpu as pltpu
from jax.sharding import PartitionSpec as P

MESH = pl.DeviceIdType.MESH
BLK = 128
RANK = 128
BR_DEV = 8
CAP = 16
SIDE = 4
HIGHEST = lax.Precision.HIGHEST


def place():
    row = lax.axis_index("row")
    return row // 8, lax.rem(row // 2, SIDE), lax.rem(row, 2), lax.axis_index("col")


def row_of(z, x, core):
    return z * 8 + x * 2 + core


def gather_kernel(mine_ref, all_ref, local_sem, send_sem, recv_sem, pair_send, pair_recv):
    z, x, core, y = place()
    rows = mine_ref.shape[0]
    half, quarter = rows // 2, rows // 4

    barrier = pltpu.get_barrier_semaphore()

    def other(dz, dx):
        return (row_of(lax.rem(z + dz + SIDE, SIDE), lax.rem(x + dx + SIDE, SIDE), core), y)

    pair = (row_of(z, x, 1 - core), y)
    for peer in (other(0, 1), other(0, -1), other(1, 0), other(-1, 0), pair):
        pl.semaphore_signal(barrier, inc=1, device_id=peer, device_id_type=MESH)
    pl.semaphore_wait(barrier, 5)

    me = row_of(z, x, core)
    own = pltpu.make_async_copy(mine_ref, all_ref.at[me], local_sem)
    own.start()

    pending = []
    index = {}

    def slot(name):
        return index.setdefault(name, len(index))

    def shift(h, along, across):
        return (across, along) if h == 0 else (along, across)

    def piece(h, a, b, part):
        dz, dx = shift(h, -a, -b)
        source = row_of(lax.rem(z + dz + SIDE, SIDE), lax.rem(x + dx + SIDE, SIDE), core)
        start, size = {"all": (h * half, half), "lo": (h * half, quarter), "hi": (h * half + quarter, quarter)}[part]
        return source, pl.ds(start, size)

    def send(h, a, b, part, axis, step):
        source, span = piece(h, a, b, part)
        to = other(*(shift(h, step, 0) if axis == 0 else shift(h, 0, step)))
        there = (h, (a + step) % SIDE, b, part) if axis == 0 else (h, a, (b + step) % SIDE, part)
        s = slot(there)
        src = mine_ref.at[span] if (a, b) == (0, 0) else all_ref.at[source, span]
        copy = pltpu.make_async_remote_copy(
            src_ref=src, dst_ref=all_ref.at[source, span], send_sem=send_sem.at[s], recv_sem=recv_sem.at[s],
            device_id=to, device_id_type=MESH,
        )
        copy.start()
        pending.append(copy)

    def arrived(h, a, b, part):
        s = slot((h, a, b, part))
        source, span = piece(h, a, b, part)
        there = all_ref.at[source, span]
        pltpu.make_async_remote_copy(
            src_ref=there, dst_ref=there, send_sem=send_sem.at[s], recv_sem=recv_sem.at[s], device_id=pair,
            device_id_type=MESH,
        ).wait_recv()

    shared = []

    def share(h, a, b, part):
        s = len(shared)
        source, span = piece(h, a, b, part)
        src = mine_ref.at[span] if (a, b) == (0, 0) else all_ref.at[source, span]
        copy = pltpu.make_async_remote_copy(
            src_ref=src, dst_ref=all_ref.at[source, span], send_sem=pair_send.at[s], recv_sem=pair_recv.at[s],
            device_id=pair, device_id_type=MESH,
        )
        copy.start()
        flip, _ = piece(h, a, b, part)
        shared.append((copy, flip + 1 - 2 * core, span))

    for h in (0, 1):
        for step in (1, -1):
            send(h, 0, 0, "all", 0, step)
    for h in (0, 1):
        for step in (1, -1):
            send(h, 0, 0, "all", 1, step)
    for h in (0, 1):
        share(h, 0, 0, "all")
    for step in (1, -1):
        for h in (0, 1):
            a = step % SIDE
            arrived(h, a, 0, "all")
            send(h, a, 0, "lo" if step == 1 else "hi", 0, step)
            for onward in (1, -1):
                send(h, a, 0, "all", 1, onward)
            share(h, a, 0, "all")
    for h in (0, 1):
        arrived(h, 2, 0, "lo")
        arrived(h, 2, 0, "hi")
        for onward in (1, -1):
            send(h, 2, 0, "all", 1, onward)
        share(h, 2, 0, "all")
    for a in (0, 1, 3, 2):
        for step in (1, -1):
            for h in (0, 1):
                arrived(h, a, step % SIDE, "all")
                send(h, a, step % SIDE, "lo" if step == 1 else "hi", 1, step)
                share(h, a, step % SIDE, "all")
    for a in (0, 1, 3, 2):
        for h in (0, 1):
            for part in ("lo", "hi"):
                arrived(h, a, 2, part)
            share(h, a, 2, "all")
    own.wait()
    for copy in pending:
        copy.wait_send()
    for s, (copy, source, span) in enumerate(shared):
        copy.wait_send()
        there = all_ref.at[source, span]
        pltpu.make_async_remote_copy(
            src_ref=there, dst_ref=there, send_sem=pair_send.at[s], recv_sem=pair_recv.at[s], device_id=pair,
            device_id_type=MESH,
        ).wait_recv()


def gather(sketch):
    return pl.pallas_call(
        gather_kernel,
        out_shape=jax.ShapeDtypeStruct((32,) + sketch.shape, sketch.dtype),
        in_specs=[pl.BlockSpec(memory_space=pl.ANY)],
        out_specs=pl.BlockSpec(memory_space=pl.ANY),
        scratch_shapes=[
            pltpu.SemaphoreType.DMA,
            pltpu.SemaphoreType.DMA((48,)),
            pltpu.SemaphoreType.DMA((48,)),
            pltpu.SemaphoreType.DMA((32,)),
            pltpu.SemaphoreType.DMA((32,)),
        ],
        compiler_params=pltpu.CompilerParams(collective_id=0, has_side_effects=True),
    )(sketch)


def products_kernel(row_ref, col_ref, blocks_ref, sketch_ref, out_ref, total_ref):
    group = pl.program_id(0)

    @pl.when(group == 0)
    def _():
        total_ref[...] = jnp.zeros_like(total_ref)

    for k in range(CAP):
        row = row_ref[group * CAP + k]
        col = jnp.maximum(col_ref[group * CAP + k], 0)
        target = jnp.where(row < 0, BR_DEV, row)
        total_ref[target] += jnp.dot(blocks_ref[k], sketch_ref[0, col], preferred_element_type=jnp.float32)

    @pl.when(group == pl.num_programs(0) - 1)
    def _():
        out_ref[...] = total_ref[pl.ds(0, BR_DEV)]


def products(blocks, block_row, block_col, gathered):
    groups = gathered.shape[0]
    per = gathered.shape[1] // BLK
    return pl.pallas_call(
        products_kernel,
        out_shape=jax.ShapeDtypeStruct((BR_DEV, BLK, RANK), jnp.float32),
        grid_spec=pltpu.PrefetchScalarGridSpec(
            num_scalar_prefetch=2,
            grid=(groups,),
            in_specs=[
                pl.BlockSpec((CAP, BLK, BLK), lambda g, *_: (g, 0, 0)),
                pl.BlockSpec((1, per, BLK, RANK), lambda g, *_: (g, 0, 0, 0)),
            ],
            out_specs=pl.BlockSpec((BR_DEV, BLK, RANK), lambda g, *_: (0, 0, 0)),
            scratch_shapes=[pltpu.VMEM((BR_DEV + 1, BLK, RANK), jnp.float32)],
        ),
        compiler_params=pltpu.CompilerParams(vmem_limit_bytes=24 * 2**20),
    )(block_row, block_col, blocks, gathered.reshape(groups, per, BLK, RANK))


def reduce_kernel(part_ref, slab_ref, gram_ref, local_ref, col_buf, pair_buf, x_buf, z_buf, col_s, col_r, pair_s, pair_r, x_s, x_r, z_s, z_r, last_s, last_r):
    z, x, core, y = place()
    rows = slab_ref.shape[0]
    strip = RANK // 8
    me8 = y * 2 + core

    def octet(step):
        number = lax.rem(me8 + step, 8)
        return (row_of(z, x, lax.rem(number, 2)), number // 2), number

    def along_x(step):
        return (row_of(z, lax.rem(x + step, SIDE), core), y)

    def along_z(step):
        return (row_of(lax.rem(z + step, SIDE), x, core), y)

    barrier = pltpu.get_barrier_semaphore()
    for step in range(1, 8):
        pl.semaphore_signal(barrier, inc=1, device_id=octet(step)[0], device_id_type=MESH)
    for step in range(1, SIDE):
        pl.semaphore_signal(barrier, inc=1, device_id=along_x(step), device_id_type=MESH)
        pl.semaphore_signal(barrier, inc=1, device_id=along_z(step), device_id_type=MESH)
    pl.semaphore_wait(barrier, 13)

    sent = []

    def push(src, dst, send, recv, to):
        copy = pltpu.make_async_remote_copy(
            src_ref=src, dst_ref=dst, send_sem=send, recv_sem=recv, device_id=to, device_id_type=MESH
        )
        copy.start()
        sent.append(copy)
        return copy

    copies = []
    for step in (2, 1, 3):
        to = lax.rem(y + step, SIDE)
        copies.append(push(
            part_ref.at[pl.ds(to * rows, rows)], col_buf.at[step - 1], col_s.at[step - 1], col_r.at[step - 1],
            (lax.axis_index("row"), to),
        ))
    total = part_ref[pl.ds(y * rows, rows), :]
    for copy in copies:
        copy.wait_recv()
    total = total + (col_buf[0] + col_buf[1] + col_buf[2])
    slab_ref[...] = total
    local_ref[...] = lax.dot_general(
        total, total, (((0,), (0,)), ((), ())), precision=HIGHEST, preferred_element_type=jnp.float32
    )

    copies = []
    for step in range(1, 8):
        to, number = octet(step)
        copies.append(push(
            local_ref.at[pl.ds(number * strip, strip)], pair_buf.at[step - 1], pair_s.at[step - 1],
            pair_r.at[step - 1], to,
        ))
    part = local_ref[pl.ds(me8 * strip, strip), :]
    for step, copy in enumerate(copies):
        copy.wait_recv()
        part = part + pair_buf[step]

    for here, buf, send, recv, peer in ((x, x_buf, x_s, x_r, along_x), (z, z_buf, z_s, z_r, along_z)):
        buf[pl.ds(here, 1)] = part[None]
        copies = []
        for step in range(1, SIDE):
            copies.append(push(buf.at[here], buf.at[here], send.at[step - 1], recv.at[step - 1], peer(step)))
        for copy in copies:
            copy.wait_recv()
        part = (buf[0] + buf[1]) + (buf[2] + buf[3])

    mine = pl.ds(me8 * strip, strip)
    gram_ref[mine, :] = part
    for step in range(1, 8):
        to, number = octet(step)
        push(gram_ref.at[mine], gram_ref.at[mine], last_s.at[step - 1], last_r.at[step - 1], to)
    for copy in sent[-7:]:
        copy.wait_recv()
    for copy in sent:
        copy.wait_send()


def reduce(partial):
    rows = partial.shape[0] // SIDE
    dma = pltpu.SemaphoreType.DMA
    strip = RANK // 8
    f32 = jnp.float32
    return pl.pallas_call(
        reduce_kernel,
        out_shape=(jax.ShapeDtypeStruct((rows, RANK), f32), jax.ShapeDtypeStruct((RANK, RANK), f32)),
        in_specs=[pl.BlockSpec(memory_space=pltpu.VMEM)],
        out_specs=(pl.BlockSpec(memory_space=pltpu.VMEM),) * 2,
        scratch_shapes=[
            pltpu.VMEM((RANK, RANK), f32),
            pltpu.VMEM((3, rows, RANK), f32),
            pltpu.VMEM((7, strip, RANK), f32),
            pltpu.VMEM((SIDE, strip, RANK), f32),
            pltpu.VMEM((SIDE, strip, RANK), f32),
            dma((3,)), dma((3,)), dma((7,)), dma((7,)), dma((3,)), dma((3,)), dma((3,)), dma((3,)), dma((7,)), dma((7,)),
        ],
        compiler_params=pltpu.CompilerParams(collective_id=1, has_side_effects=True),
    )(partial)


def factor_kernel(gram_ref, slab_ref, basis_ref, factor_ref):
    tile = (8, RANK)
    count = RANK // 8
    lane = lax.broadcasted_iota(jnp.int32, tile, 1)
    sub = lax.broadcasted_iota(jnp.int32, tile, 0)
    left = [gram_ref[8 * i : 8 * i + 8, :] for i in range(count)]
    right = [jnp.where(lane == sub + 8 * i, 1.0, 0.0) for i in range(count)]
    inverse = []
    for p in range(count):
        cols = {
            (i, m): jnp.broadcast_to(left[i][:, 8 * p + m : 8 * p + m + 1], tile)
            for i in range(p, count)
            for m in range(8)
        }
        upper = jnp.zeros(tile, jnp.float32)
        lower = jnp.zeros(tile, jnp.float32)
        for k in range(8):
            pivot = jnp.broadcast_to(cols[p, k][k : k + 1, :], tile)
            scale = lax.rsqrt(pivot)
            row = jnp.broadcast_to(left[p][k : k + 1, :], tile) * scale
            inverse_row = jnp.broadcast_to(right[p][k : k + 1, :], tile) * scale
            upper = jnp.where(sub == k, row, upper)
            lower = jnp.where(sub == k, inverse_row, lower)
            ahead = {m: jnp.broadcast_to(cols[p, m][k : k + 1, :], tile) * scale for m in range(k + 1, 8)}
            for i in range(p, count):
                if i == p and k == 7:
                    continue
                weight = cols[i, k] * scale
                for m in range(k + 1, 8):
                    cols[i, m] = cols[i, m] - weight * ahead[m]
                left[i] = left[i] - weight * row
                right[i] = right[i] - weight * inverse_row
        factor_ref[8 * p : 8 * p + 8, :] = jnp.where(lane >= sub + 8 * p, upper, 0.0)
        inverse.append(lower)
    basis_ref[...] = lax.dot_general(
        slab_ref[...],
        jnp.concatenate(inverse, axis=0),
        (((1,), (1,)), ((), ())),
        precision=HIGHEST,
        preferred_element_type=jnp.float32,
    )


def factorise(gram, slab):
    return pl.pallas_call(
        factor_kernel,
        out_shape=(
            jax.ShapeDtypeStruct(slab.shape, jnp.float32),
            jax.ShapeDtypeStruct(gram.shape, jnp.float32),
        ),
    )(gram, slab)


def shards(blocks, block_row, block_col, sketch):
    gathered = gather(sketch)
    partial = products(blocks, block_row, block_col, gathered)
    slab, gram = reduce(partial.reshape(BR_DEV * BLK, RANK))
    return factorise(gram, slab)


def solution(mesh):
    in_specs = (
        P(("row", "col"), None, None),
        P(("row", "col")),
        P(("row", "col")),
        P(("row", "col"), None),
    )
    out_specs = (P(("row", "col"), None), P())
    return jax.shard_map(shards, mesh=mesh, in_specs=in_specs, out_specs=out_specs, check_vma=False)
```

```python
import functools

import jax
import jax.numpy as jnp
from jax import lax
from jax.experimental import pallas as pl
from jax.experimental.pallas import tpu as pltpu
from jax.sharding import PartitionSpec as P

MESH = pl.DeviceIdType.MESH
BLK = 128
RANK = 128
BR_DEV = 8
CAP = 16
SIDE = 4
HIGHEST = lax.Precision.HIGHEST


def place():
    row = lax.axis_index("row")
    return row // 8, lax.rem(row // 2, SIDE), lax.rem(row, 2), lax.axis_index("col")


def row_of(z, x, core):
    return z * 8 + x * 2 + core


TURNS = (
    (),
    ((0, 1), (1, 0)),
    ((0, 3),),
    ((3, 0),),
    ((1, 1),),
    ((1, 3),),
    ((3, 1),),
    ((3, 3),),
    (),
    ((0, 2), (2, 0)),
    ((1, 2), (2, 1)),
    ((3, 2), (2, 3)),
)


def sampled_kernel(row_ref, col_ref, blocks_ref, mine_ref, total_ref, *scratch):
    held = {(c // SIDE, c % SIDE): scratch[c] for c in range(SIDE * SIDE)}
    stored, chain, block_sem, own_sem, send_sem, recv_sem, pair_send, pair_recv = scratch[SIDE * SIDE :]
    z, x, core, y = place()
    count = mine_ref.shape[0]
    half, quarter = count // 2, count // 4

    barrier = pltpu.get_barrier_semaphore()

    def other(dz, dx):
        return (row_of(lax.rem(z + dz + SIDE, SIDE), lax.rem(x + dx + SIDE, SIDE), core), y)

    pair = (row_of(z, x, 1 - core), y)
    for peer in (other(0, 1), other(0, -1), other(1, 0), other(-1, 0), pair):
        pl.semaphore_signal(barrier, inc=1, device_id=peer, device_id_type=MESH)
    own = pltpu.make_async_copy(mine_ref, held[0, 0].at[0], own_sem)
    own.start()
    store = pltpu.make_async_copy(blocks_ref, stored, block_sem)
    pl.semaphore_wait(barrier, 5)

    pending = []
    index = {}

    def spot(h, a, b, part, plane):
        start, size = {"all": (h * half, half), "lo": (h * half, quarter), "hi": (h * half + quarter, quarter)}[part]
        return held[(a, b) if h == 0 else (b, a)].at[plane, pl.ds(start, size)]

    def origin(h, a, b, part):
        if (a, b) == (0, 0):
            return mine_ref.at[pl.ds(h * half, half)]
        return spot(h, a, b, part, 0)

    def send(h, a, b, part, axis, step):
        shift = (step, 0) if axis == 0 else (0, step)
        there = (h, (a + shift[0]) % SIDE, (b + shift[1]) % SIDE, part)
        s = index.setdefault(there, len(index))
        copy = pltpu.make_async_remote_copy(
            src_ref=origin(h, a, b, part), dst_ref=spot(*there, 0), send_sem=send_sem.at[s], recv_sem=recv_sem.at[s],
            device_id=other(*(shift[::-1] if h == 0 else shift)), device_id_type=MESH,
        )
        copy.start()
        pending.append(copy)

    def arrived(h, a, b, part):
        s = index[h, a, b, part]
        there = spot(h, a, b, part, 0)
        pltpu.make_async_remote_copy(
            src_ref=there, dst_ref=there, send_sem=send_sem.at[s], recv_sem=recv_sem.at[s], device_id=pair,
            device_id_type=MESH,
        ).wait_recv()

    shared = {}

    def share(h, a, b):
        s = len(shared)
        copy = pltpu.make_async_remote_copy(
            src_ref=origin(h, a, b, "all"), dst_ref=spot(h, a, b, "all", 1), send_sem=pair_send.at[s],
            recv_sem=pair_recv.at[s], device_id=pair, device_id_type=MESH,
        )
        copy.start()
        pending.append(copy)
        shared[h, a, b] = copy

    def multiply(dx, dz):
        shared[0, dx, dz].wait_recv()
        shared[1, dz, dx].wait_recv()
        sketch = held[dx, dz]

        def one_group(plane, _):
            group = row_of(lax.rem(z - dz + SIDE, SIDE), lax.rem(x - dx + SIDE, SIDE), lax.rem(core + plane, 2))
            last = [CAP] * BR_DEV
            for k in range(CAP):
                row = row_ref[group * CAP + k]
                col = jnp.maximum(col_ref[group * CAP + k], 0)
                before = CAP
                for b in range(BR_DEV):
                    same = row == b
                    before = jnp.where(same, last[b], before)
                    last[b] = jnp.where(same, k, last[b])
                product = jnp.dot(stored[group, k], sketch[plane, col], preferred_element_type=jnp.float32)
                chain[k] = product + chain[before]
            for b in range(BR_DEV):
                total_ref[b] += chain[last[b]]
            return 0

        lax.fori_loop(0, 2, one_group, 0)

    for h in (0, 1):
        for step in (1, -1):
            send(h, 0, 0, "all", 0, step)
    for h in (0, 1):
        share(h, 0, 0)
    for h in (0, 1):
        for step in (1, -1):
            send(h, 0, 0, "all", 1, step)
    store.start()
    total_ref[...] = jnp.zeros_like(total_ref)
    chain[CAP] = jnp.zeros_like(chain[CAP])
    own.wait()
    store.wait()
    multiply(0, 0)
    for step in (1, -1):
        for h in (0, 1):
            a = step % SIDE
            arrived(h, a, 0, "all")
            send(h, a, 0, "lo" if step == 1 else "hi", 0, step)
            for onward in (1, -1):
                send(h, a, 0, "all", 1, onward)
            share(h, a, 0)
    for h in (0, 1):
        arrived(h, 2, 0, "lo")
        arrived(h, 2, 0, "hi")
        for onward in (1, -1):
            send(h, 2, 0, "all", 1, onward)
        share(h, 2, 0)
    turns = iter(TURNS)
    for a in (0, 1, 3, 2):
        for step in (1, -1):
            for h in (0, 1):
                arrived(h, a, step % SIDE, "all")
                send(h, a, step % SIDE, "lo" if step == 1 else "hi", 1, step)
                share(h, a, step % SIDE)
            for chip in next(turns):
                multiply(*chip)
    for a in (0, 1, 3, 2):
        for h in (0, 1):
            for part in ("lo", "hi"):
                arrived(h, a, 2, part)
            share(h, a, 2)
        for chip in next(turns):
            multiply(*chip)
    multiply(2, 2)
    for copy in pending:
        copy.wait_send()


def sample(blocks, block_row, block_col, sketch):
    groups = blocks.shape[0] // CAP
    count = sketch.shape[0] // BLK
    dma = pltpu.SemaphoreType.DMA
    return pl.pallas_call(
        sampled_kernel,
        out_shape=jax.ShapeDtypeStruct((BR_DEV, BLK, RANK), jnp.float32),
        in_specs=[
            pl.BlockSpec(memory_space=pltpu.SMEM),
            pl.BlockSpec(memory_space=pltpu.SMEM),
            pl.BlockSpec(memory_space=pl.ANY),
            pl.BlockSpec(memory_space=pl.ANY),
        ],
        out_specs=pl.BlockSpec(memory_space=pltpu.VMEM),
        scratch_shapes=[pltpu.VMEM((2, count, BLK, RANK), sketch.dtype)] * (SIDE * SIDE)
        + [
            pltpu.VMEM((groups, CAP, BLK, BLK), blocks.dtype),
            pltpu.VMEM((CAP + 1, BLK, RANK), jnp.float32),
            dma,
            dma,
            dma((48,)),
            dma((48,)),
            dma((32,)),
            dma((32,)),
        ],
        compiler_params=pltpu.CompilerParams(
            collective_id=0, has_side_effects=True, vmem_limit_bytes=58 * 2**20
        ),
    )(block_row, block_col, blocks.reshape(groups, CAP, BLK, BLK), sketch.reshape(count, BLK, RANK))


def reduce_kernel(part_ref, slab_ref, gram_ref, local_ref, col_buf, pair_buf, x_buf, z_buf, col_s, col_r, pair_s, pair_r, x_s, x_r, z_s, z_r, last_s, last_r):
    z, x, core, y = place()
    rows = slab_ref.shape[0]
    strip = RANK // 8
    me8 = y * 2 + core

    def octet(step):
        number = lax.rem(me8 + step, 8)
        return (row_of(z, x, lax.rem(number, 2)), number // 2), number

    def along_x(step):
        return (row_of(z, lax.rem(x + step, SIDE), core), y)

    def along_z(step):
        return (row_of(lax.rem(z + step, SIDE), x, core), y)

    barrier = pltpu.get_barrier_semaphore()
    for step in range(1, 8):
        pl.semaphore_signal(barrier, inc=1, device_id=octet(step)[0], device_id_type=MESH)
    for step in range(1, SIDE):
        pl.semaphore_signal(barrier, inc=1, device_id=along_x(step), device_id_type=MESH)
        pl.semaphore_signal(barrier, inc=1, device_id=along_z(step), device_id_type=MESH)
    pl.semaphore_wait(barrier, 13)

    sent = []

    def push(src, dst, send, recv, to):
        copy = pltpu.make_async_remote_copy(
            src_ref=src, dst_ref=dst, send_sem=send, recv_sem=recv, device_id=to, device_id_type=MESH
        )
        copy.start()
        sent.append(copy)
        return copy

    copies = []
    for step in (2, 1, 3):
        to = lax.rem(y + step, SIDE)
        copies.append(push(
            part_ref.at[pl.ds(to * rows, rows)], col_buf.at[step - 1], col_s.at[step - 1], col_r.at[step - 1],
            (lax.axis_index("row"), to),
        ))
    total = part_ref[pl.ds(y * rows, rows), :]
    for copy in copies:
        copy.wait_recv()
    total = total + (col_buf[0] + col_buf[1] + col_buf[2])
    slab_ref[...] = total
    local_ref[...] = lax.dot_general(
        total, total, (((0,), (0,)), ((), ())), precision=HIGHEST, preferred_element_type=jnp.float32
    )

    copies = []
    for step in range(1, 8):
        to, number = octet(step)
        copies.append(push(
            local_ref.at[pl.ds(number * strip, strip)], pair_buf.at[step - 1], pair_s.at[step - 1],
            pair_r.at[step - 1], to,
        ))
    part = local_ref[pl.ds(me8 * strip, strip), :]
    for step, copy in enumerate(copies):
        copy.wait_recv()
        part = part + pair_buf[step]

    for here, buf, send, recv, peer in ((x, x_buf, x_s, x_r, along_x), (z, z_buf, z_s, z_r, along_z)):
        buf[pl.ds(here, 1)] = part[None]
        copies = []
        for step in range(1, SIDE):
            copies.append(push(buf.at[here], buf.at[here], send.at[step - 1], recv.at[step - 1], peer(step)))
        for copy in copies:
            copy.wait_recv()
        part = (buf[0] + buf[1]) + (buf[2] + buf[3])

    mine = pl.ds(me8 * strip, strip)
    gram_ref[mine, :] = part
    for step in range(1, 8):
        to, number = octet(step)
        push(gram_ref.at[mine], gram_ref.at[mine], last_s.at[step - 1], last_r.at[step - 1], to)
    for copy in sent[-7:]:
        copy.wait_recv()
    for copy in sent:
        copy.wait_send()


def reduce(partial):
    rows = partial.shape[0] // SIDE
    dma = pltpu.SemaphoreType.DMA
    strip = RANK // 8
    f32 = jnp.float32
    return pl.pallas_call(
        reduce_kernel,
        out_shape=(jax.ShapeDtypeStruct((rows, RANK), f32), jax.ShapeDtypeStruct((RANK, RANK), f32)),
        in_specs=[pl.BlockSpec(memory_space=pltpu.VMEM)],
        out_specs=(pl.BlockSpec(memory_space=pltpu.VMEM),) * 2,
        scratch_shapes=[
            pltpu.VMEM((RANK, RANK), f32),
            pltpu.VMEM((3, rows, RANK), f32),
            pltpu.VMEM((7, strip, RANK), f32),
            pltpu.VMEM((SIDE, strip, RANK), f32),
            pltpu.VMEM((SIDE, strip, RANK), f32),
            dma((3,)), dma((3,)), dma((7,)), dma((7,)), dma((3,)), dma((3,)), dma((3,)), dma((3,)), dma((7,)), dma((7,)),
        ],
        compiler_params=pltpu.CompilerParams(collective_id=1, has_side_effects=True),
    )(partial)


def factor_kernel(gram_ref, slab_ref, basis_ref, factor_ref):
    tile = (8, RANK)
    count = RANK // 8
    lane = lax.broadcasted_iota(jnp.int32, tile, 1)
    sub = lax.broadcasted_iota(jnp.int32, tile, 0)
    left = [gram_ref[8 * i : 8 * i + 8, :] for i in range(count)]
    right = [jnp.where(lane == sub + 8 * i, 1.0, 0.0) for i in range(count)]
    inverse = []
    for p in range(count):
        cols = {
            (i, m): jnp.broadcast_to(left[i][:, 8 * p + m : 8 * p + m + 1], tile)
            for i in range(p, count)
            for m in range(8)
        }
        upper = jnp.zeros(tile, jnp.float32)
        lower = jnp.zeros(tile, jnp.float32)
        for k in range(8):
            pivot = jnp.broadcast_to(cols[p, k][k : k + 1, :], tile)
            scale = lax.rsqrt(pivot)
            row = jnp.broadcast_to(left[p][k : k + 1, :], tile) * scale
            inverse_row = jnp.broadcast_to(right[p][k : k + 1, :], tile) * scale
            upper = jnp.where(sub == k, row, upper)
            lower = jnp.where(sub == k, inverse_row, lower)
            ahead = {m: jnp.broadcast_to(cols[p, m][k : k + 1, :], tile) * scale for m in range(k + 1, 8)}
            for i in range(p, count):
                if i == p and k == 7:
                    continue
                weight = cols[i, k] * scale
                for m in range(k + 1, 8):
                    cols[i, m] = cols[i, m] - weight * ahead[m]
                left[i] = left[i] - weight * row
                right[i] = right[i] - weight * inverse_row
        factor_ref[8 * p : 8 * p + 8, :] = jnp.where(lane >= sub + 8 * p, upper, 0.0)
        inverse.append(lower)
    basis_ref[...] = lax.dot_general(
        slab_ref[...],
        jnp.concatenate(inverse, axis=0),
        (((1,), (1,)), ((), ())),
        precision=HIGHEST,
        preferred_element_type=jnp.float32,
    )


def factorise(gram, slab):
    return pl.pallas_call(
        factor_kernel,
        out_shape=(
            jax.ShapeDtypeStruct(slab.shape, jnp.float32),
            jax.ShapeDtypeStruct(gram.shape, jnp.float32),
        ),
    )(gram, slab)


def shards(blocks, block_row, block_col, sketch):
    partial = sample(blocks, block_row, block_col, sketch)
    slab, gram = reduce(partial.reshape(BR_DEV * BLK, RANK))
    return factorise(gram, slab)


def solution(mesh):
    in_specs = (
        P(("row", "col"), None, None),
        P(("row", "col")),
        P(("row", "col")),
        P(("row", "col"), None),
    )
    out_specs = (P(("row", "col"), None), P())
    return jax.shard_map(shards, mesh=mesh, in_specs=in_specs, out_specs=out_specs, check_vma=False)
```

```python
import functools

import jax
import jax.numpy as jnp
from jax import lax
from jax.experimental import pallas as pl
from jax.experimental.pallas import tpu as pltpu
from jax.sharding import PartitionSpec as P

MESH = pl.DeviceIdType.MESH
BLK = 128
RANK = 128
BR_DEV = 8
CAP = 16
SIDE = 4
HIGHEST = lax.Precision.HIGHEST


def place():
    row = lax.axis_index("row")
    return row // 8, lax.rem(row // 2, SIDE), lax.rem(row, 2), lax.axis_index("col")


def row_of(z, x, core):
    return z * 8 + x * 2 + core


def far(step):
    return sum(min(d, SIDE - d) for d in step)


TURNS = (
    (),
    ((0, 1), (1, 0)),
    ((0, 3),),
    ((3, 0),),
    ((1, 1),),
    ((1, 3),),
    ((3, 1),),
    ((3, 3),),
    (),
    ((0, 2), (2, 0)),
    ((1, 2), (2, 1)),
    ((3, 2), (2, 3)),
)


def sampled_kernel(row_ref, col_ref, blocks_ref, mine_ref, slab_ref, gram_ref, *scratch):
    held = {(c // SIDE, c % SIDE): scratch[c] for c in range(SIDE * SIDE)}
    stored, chain, total_ref, local_ref, col_buf, octet_buf, plane_buf, *scratch = scratch[SIDE * SIDE :]
    block_sem, own_sem, send_sem, recv_sem, pair_send, pair_recv, *scratch = scratch
    col_send, col_recv, octet_send, octet_recv, plane_send, plane_recv, last_send, last_recv = scratch
    z, x, core, y = place()
    count = mine_ref.shape[0]
    half, quarter = count // 2, count // 4

    barrier = pltpu.get_barrier_semaphore()

    def other(dz, dx):
        return (row_of(lax.rem(z + dz + SIDE, SIDE), lax.rem(x + dx + SIDE, SIDE), core), y)

    me8 = y * 2 + core

    def octet(step):
        number = lax.rem(me8 + step, 8)
        return (row_of(z, x, lax.rem(number, 2)), number // 2), number

    pair = (row_of(z, x, 1 - core), y)
    for peer in (other(0, 1), other(0, -1), other(1, 0), other(-1, 0), *(octet(step)[0] for step in range(1, 8))):
        pl.semaphore_signal(barrier, inc=1, device_id=peer, device_id_type=MESH)
    own = pltpu.make_async_copy(mine_ref, held[0, 0].at[0], own_sem)
    own.start()
    store = pltpu.make_async_copy(blocks_ref, stored, block_sem)
    pl.semaphore_wait(barrier, 11)

    pending = []
    index = {}

    def spot(h, a, b, part, plane):
        start, size = {"all": (h * half, half), "lo": (h * half, quarter), "hi": (h * half + quarter, quarter)}[part]
        return held[(a, b) if h == 0 else (b, a)].at[plane, pl.ds(start, size)]

    def origin(h, a, b, part):
        if (a, b) == (0, 0):
            return mine_ref.at[pl.ds(h * half, half)]
        return spot(h, a, b, part, 0)

    def send(h, a, b, part, axis, step):
        shift = (step, 0) if axis == 0 else (0, step)
        there = (h, (a + shift[0]) % SIDE, (b + shift[1]) % SIDE, part)
        s = index.setdefault(there, len(index))
        copy = pltpu.make_async_remote_copy(
            src_ref=origin(h, a, b, part), dst_ref=spot(*there, 0), send_sem=send_sem.at[s], recv_sem=recv_sem.at[s],
            device_id=other(*(shift[::-1] if h == 0 else shift)), device_id_type=MESH,
        )
        copy.start()
        pending.append(copy)

    def arrived(h, a, b, part):
        s = index[h, a, b, part]
        there = spot(h, a, b, part, 0)
        pltpu.make_async_remote_copy(
            src_ref=there, dst_ref=there, send_sem=send_sem.at[s], recv_sem=recv_sem.at[s], device_id=pair,
            device_id_type=MESH,
        ).wait_recv()

    shared = {}

    def share(h, a, b):
        s = len(shared)
        copy = pltpu.make_async_remote_copy(
            src_ref=origin(h, a, b, "all"), dst_ref=spot(h, a, b, "all", 1), send_sem=pair_send.at[s],
            recv_sem=pair_recv.at[s], device_id=pair, device_id_type=MESH,
        )
        copy.start()
        pending.append(copy)
        shared[h, a, b] = copy

    def multiply(dx, dz):
        shared[0, dx, dz].wait_recv()
        shared[1, dz, dx].wait_recv()
        sketch = held[dx, dz]

        def one_group(plane, _):
            group = row_of(lax.rem(z - dz + SIDE, SIDE), lax.rem(x - dx + SIDE, SIDE), lax.rem(core + plane, 2))
            last = [CAP] * BR_DEV
            for k in range(CAP):
                row = row_ref[group * CAP + k]
                col = jnp.maximum(col_ref[group * CAP + k], 0)
                before = CAP
                for b in range(BR_DEV):
                    same = row == b
                    before = jnp.where(same, last[b], before)
                    last[b] = jnp.where(same, k, last[b])
                product = jnp.dot(stored[group, k], sketch[plane, col], preferred_element_type=jnp.float32)
                chain[k] = product + chain[before]
            for b in range(BR_DEV):
                total_ref[b] += chain[last[b]]
            return 0

        lax.fori_loop(0, 2, one_group, 0)

    for h in (0, 1):
        for step in (1, -1):
            send(h, 0, 0, "all", 0, step)
    for h in (0, 1):
        share(h, 0, 0)
    for h in (0, 1):
        for step in (1, -1):
            send(h, 0, 0, "all", 1, step)
    store.start()
    total_ref[...] = jnp.zeros_like(total_ref)
    chain[CAP] = jnp.zeros_like(chain[CAP])
    own.wait()
    store.wait()
    multiply(0, 0)
    for step in (1, -1):
        for h in (0, 1):
            a = step % SIDE
            arrived(h, a, 0, "all")
            send(h, a, 0, "lo" if step == 1 else "hi", 0, step)
            for onward in (1, -1):
                send(h, a, 0, "all", 1, onward)
            share(h, a, 0)
    for h in (0, 1):
        arrived(h, 2, 0, "lo")
        arrived(h, 2, 0, "hi")
        for onward in (1, -1):
            send(h, 2, 0, "all", 1, onward)
        share(h, 2, 0)
    turns = iter(TURNS)
    for a in (0, 1, 3, 2):
        for step in (1, -1):
            for h in (0, 1):
                arrived(h, a, step % SIDE, "all")
                send(h, a, step % SIDE, "lo" if step == 1 else "hi", 1, step)
                share(h, a, step % SIDE)
            for chip in next(turns):
                multiply(*chip)
    for a in (0, 1, 3, 2):
        for h in (0, 1):
            for part in ("lo", "hi"):
                arrived(h, a, 2, part)
            share(h, a, 2)
        for chip in next(turns):
            multiply(*chip)
    multiply(2, 2)

    def push(src, dst, send_to, recv_from, peer):
        copy = pltpu.make_async_remote_copy(
            src_ref=src, dst_ref=dst, send_sem=send_to, recv_sem=recv_from, device_id=peer, device_id_type=MESH
        )
        copy.start()
        pending.append(copy)
        return copy

    share_rows = BR_DEV // SIDE
    copies = []
    for step in (2, 1, 3):
        to = lax.rem(y + step, SIDE)
        copies.append(push(
            total_ref.at[pl.ds(to * share_rows, share_rows)], col_buf.at[step - 1], col_send.at[step - 1],
            col_recv.at[step - 1], (lax.axis_index("row"), to),
        ))
    slab = total_ref[pl.ds(y * share_rows, share_rows)]
    for copy in copies:
        copy.wait_recv()
    slab = (slab + (col_buf[0] + col_buf[1] + col_buf[2])).reshape(slab_ref.shape)
    slab_ref[...] = slab
    local_ref[...] = lax.dot_general(
        slab, slab, (((0,), (0,)), ((), ())), precision=HIGHEST, preferred_element_type=jnp.float32
    )

    strip = RANK // 8
    mine = pl.ds(me8 * strip, strip)
    copies = []
    for step in (4, 5, 3, 2, 6, 1, 7):
        peer, number = octet(step)
        copies.append(push(
            local_ref.at[pl.ds(number * strip, strip)], octet_buf.at[step - 1], octet_send.at[step - 1],
            octet_recv.at[step - 1], peer,
        ))
    for copy in copies:
        copy.wait_recv()
    part = local_ref[mine, :] + jnp.sum(octet_buf[...], axis=0)
    me16 = z * SIDE + x
    plane_buf[pl.ds(me16, 1)] = part[None]
    copies = []
    for dz, dx in sorted(((a, b) for a in range(SIDE) for b in range(SIDE) if a + b), key=far, reverse=True):
        s = dz * SIDE + dx - 1
        peer = other(dz, dx)
        copies.append(push(plane_buf.at[me16], plane_buf.at[me16], plane_send.at[s], plane_recv.at[s], peer))
    for copy in copies:
        copy.wait_recv()
    gram_ref[mine, :] = jnp.sum(plane_buf[...], axis=0)
    copies = []
    for step in (4, 5, 3, 2, 6, 1, 7):
        peer, _ = octet(step)
        copies.append(push(
            gram_ref.at[mine], gram_ref.at[mine], last_send.at[step - 1], last_recv.at[step - 1], peer
        ))
    for copy in copies:
        copy.wait_recv()
    for copy in pending:
        copy.wait_send()


def sample(blocks, block_row, block_col, sketch):
    groups = blocks.shape[0] // CAP
    count = sketch.shape[0] // BLK
    dma, f32 = pltpu.SemaphoreType.DMA, jnp.float32
    return pl.pallas_call(
        sampled_kernel,
        out_shape=(
            jax.ShapeDtypeStruct((BR_DEV * BLK // SIDE, RANK), f32),
            jax.ShapeDtypeStruct((RANK, RANK), f32),
        ),
        in_specs=[
            pl.BlockSpec(memory_space=pltpu.SMEM),
            pl.BlockSpec(memory_space=pltpu.SMEM),
            pl.BlockSpec(memory_space=pl.ANY),
            pl.BlockSpec(memory_space=pl.ANY),
        ],
        out_specs=(pl.BlockSpec(memory_space=pltpu.VMEM),) * 2,
        scratch_shapes=[pltpu.VMEM((2, count, BLK, RANK), sketch.dtype)] * (SIDE * SIDE)
        + [
            pltpu.VMEM((groups, CAP, BLK, BLK), blocks.dtype),
            pltpu.VMEM((CAP + 1, BLK, RANK), f32),
            pltpu.VMEM((BR_DEV, BLK, RANK), f32),
            pltpu.VMEM((RANK, RANK), f32),
            pltpu.VMEM((SIDE - 1, BR_DEV // SIDE, BLK, RANK), f32),
            pltpu.VMEM((7, RANK // 8, RANK), f32),
            pltpu.VMEM((SIDE * SIDE, RANK // 8, RANK), f32),
            dma,
            dma,
            dma((48,)),
            dma((48,)),
            dma((32,)),
            dma((32,)),
            dma((3,)),
            dma((3,)),
            dma((7,)),
            dma((7,)),
            dma((15,)),
            dma((15,)),
            dma((7,)),
            dma((7,)),
        ],
        compiler_params=pltpu.CompilerParams(
            collective_id=0, has_side_effects=True, vmem_limit_bytes=58 * 2**20
        ),
    )(block_row, block_col, blocks.reshape(groups, CAP, BLK, BLK), sketch.reshape(count, BLK, RANK))


def factor_kernel(gram_ref, slab_ref, basis_ref, factor_ref):
    tile = (8, RANK)
    count = RANK // 8
    lane = lax.broadcasted_iota(jnp.int32, tile, 1)
    sub = lax.broadcasted_iota(jnp.int32, tile, 0)
    left = [gram_ref[8 * i : 8 * i + 8, :] for i in range(count)]
    right = [jnp.where(lane == sub + 8 * i, 1.0, 0.0) for i in range(count)]
    inverse = []
    for p in range(count):
        cols = {
            (i, m): jnp.broadcast_to(left[i][:, 8 * p + m : 8 * p + m + 1], tile)
            for i in range(p, count)
            for m in range(8)
        }
        upper = jnp.zeros(tile, jnp.float32)
        lower = jnp.zeros(tile, jnp.float32)
        for k in range(8):
            pivot = jnp.broadcast_to(cols[p, k][k : k + 1, :], tile)
            scale = lax.rsqrt(pivot)
            row = jnp.broadcast_to(left[p][k : k + 1, :], tile) * scale
            inverse_row = jnp.broadcast_to(right[p][k : k + 1, :], tile) * scale
            upper = jnp.where(sub == k, row, upper)
            lower = jnp.where(sub == k, inverse_row, lower)
            ahead = {m: jnp.broadcast_to(cols[p, m][k : k + 1, :], tile) * scale for m in range(k + 1, 8)}
            for i in range(p, count):
                if i == p and k == 7:
                    continue
                weight = cols[i, k] * scale
                for m in range(k + 1, 8):
                    cols[i, m] = cols[i, m] - weight * ahead[m]
                left[i] = left[i] - weight * row
                right[i] = right[i] - weight * inverse_row
        factor_ref[8 * p : 8 * p + 8, :] = jnp.where(lane >= sub + 8 * p, upper, 0.0)
        inverse.append(lower)
    basis_ref[...] = lax.dot_general(
        slab_ref[...],
        jnp.concatenate(inverse, axis=0),
        (((1,), (1,)), ((), ())),
        precision=HIGHEST,
        preferred_element_type=jnp.float32,
    )


def factorise(gram, slab):
    return pl.pallas_call(
        factor_kernel,
        out_shape=(
            jax.ShapeDtypeStruct(slab.shape, jnp.float32),
            jax.ShapeDtypeStruct(gram.shape, jnp.float32),
        ),
    )(gram, slab)


def shards(blocks, block_row, block_col, sketch):
    slab, gram = sample(blocks, block_row, block_col, sketch)
    return factorise(gram, slab)


def solution(mesh):
    in_specs = (
        P(("row", "col"), None, None),
        P(("row", "col")),
        P(("row", "col")),
        P(("row", "col"), None),
    )
    out_specs = (P(("row", "col"), None), P())
    return jax.shard_map(shards, mesh=mesh, in_specs=in_specs, out_specs=out_specs, check_vma=False)
```

```python
import functools

import jax
import jax.numpy as jnp
from jax import lax
from jax.experimental import pallas as pl
from jax.experimental.pallas import tpu as pltpu
from jax.sharding import PartitionSpec as P

MESH = pl.DeviceIdType.MESH
BLK = 128
RANK = 128
BR_DEV = 8
CAP = 16
SHIFT = 5
SIDE = 4
HIGHEST = lax.Precision.HIGHEST


def place():
    row = lax.axis_index("row")
    return row // 8, lax.rem(row // 2, SIDE), lax.rem(row, 2), lax.axis_index("col")


def row_of(z, x, core):
    return z * 8 + x * 2 + core


def far(step):
    return sum(min(d, SIDE - d) for d in step)


TURNS = (
    (),
    ((0, 1), (1, 0)),
    ((0, 3),),
    ((3, 0),),
    ((1, 1),),
    ((1, 3),),
    ((3, 1),),
    ((3, 3),),
    (),
    ((0, 2), (2, 0)),
    ((1, 2), (2, 1)),
    ((3, 2), (2, 3)),
)


def sampled_kernel(slot_ref, blocks_ref, mine_ref, slab_ref, gram_ref, *scratch):
    held = {(c // SIDE, c % SIDE): scratch[c] for c in range(SIDE * SIDE)}
    stored, chain, total_ref, local_ref, col_buf, octet_buf, plane_buf, *scratch = scratch[SIDE * SIDE :]
    block_sem, own_sem, send_sem, recv_sem, pair_send, pair_recv, *scratch = scratch
    col_send, col_recv, octet_send, octet_recv, plane_send, plane_recv, last_send, last_recv = scratch
    z, x, core, y = place()
    count = mine_ref.shape[0]
    half, quarter = count // 2, count // 4

    barrier = pltpu.get_barrier_semaphore()

    def other(dz, dx):
        return (row_of(lax.rem(z + dz + SIDE, SIDE), lax.rem(x + dx + SIDE, SIDE), core), y)

    me8 = y * 2 + core

    def octet(step):
        number = lax.rem(me8 + step, 8)
        return (row_of(z, x, lax.rem(number, 2)), number // 2), number

    pair = (row_of(z, x, 1 - core), y)
    for peer in (other(0, 1), other(0, -1), other(1, 0), other(-1, 0), *(octet(step)[0] for step in range(1, 8))):
        pl.semaphore_signal(barrier, inc=1, device_id=peer, device_id_type=MESH)
    own = pltpu.make_async_copy(mine_ref, held[0, 0].at[0], own_sem)
    own.start()
    store = pltpu.make_async_copy(blocks_ref, stored, block_sem)
    pl.semaphore_wait(barrier, 11)

    pending = []
    index = {}

    def spot(h, a, b, part, plane):
        start, size = {"all": (h * half, half), "lo": (h * half, quarter), "hi": (h * half + quarter, quarter)}[part]
        return held[(a, b) if h == 0 else (b, a)].at[plane, pl.ds(start, size)]

    def origin(h, a, b, part):
        if (a, b) == (0, 0):
            return mine_ref.at[pl.ds(h * half, half)]
        return spot(h, a, b, part, 0)

    def send(h, a, b, part, axis, step):
        shift = (step, 0) if axis == 0 else (0, step)
        there = (h, (a + shift[0]) % SIDE, (b + shift[1]) % SIDE, part)
        s = index.setdefault(there, len(index))
        copy = pltpu.make_async_remote_copy(
            src_ref=origin(h, a, b, part), dst_ref=spot(*there, 0), send_sem=send_sem.at[s], recv_sem=recv_sem.at[s],
            device_id=other(*(shift[::-1] if h == 0 else shift)), device_id_type=MESH,
        )
        copy.start()
        pending.append(copy)

    def arrived(h, a, b, part):
        s = index[h, a, b, part]
        there = spot(h, a, b, part, 0)
        pltpu.make_async_remote_copy(
            src_ref=there, dst_ref=there, send_sem=send_sem.at[s], recv_sem=recv_sem.at[s], device_id=pair,
            device_id_type=MESH,
        ).wait_recv()

    shared = {}

    def share(h, a, b):
        s = len(shared)
        copy = pltpu.make_async_remote_copy(
            src_ref=origin(h, a, b, "all"), dst_ref=spot(h, a, b, "all", 1), send_sem=pair_send.at[s],
            recv_sem=pair_recv.at[s], device_id=pair, device_id_type=MESH,
        )
        copy.start()
        pending.append(copy)
        shared[h, a, b] = copy

    def multiply(dx, dz):
        shared[0, dx, dz].wait_recv()
        shared[1, dz, dx].wait_recv()
        sketch = held[dx, dz]

        def one_group(plane, _):
            group = row_of(lax.rem(z - dz + SIDE, SIDE), lax.rem(x - dx + SIDE, SIDE), lax.rem(core + plane, 2))
            last = [CAP] * BR_DEV
            for k in range(CAP):
                code = slot_ref[group * CAP + k]
                row, col = code >> SHIFT, code & (2**SHIFT - 1)
                before = CAP
                for b in range(BR_DEV):
                    same = row == b
                    before = jnp.where(same, last[b], before)
                    last[b] = jnp.where(same, k, last[b])
                product = jnp.dot(stored[group, k], sketch[plane, col], preferred_element_type=jnp.float32)
                chain[k] = product + chain[before]
            for b in range(BR_DEV):
                total_ref[b] += chain[last[b]]
            return 0

        lax.fori_loop(0, 2, one_group, 0)

    for h in (0, 1):
        for step in (1, -1):
            send(h, 0, 0, "all", 0, step)
    for h in (0, 1):
        share(h, 0, 0)
    for h in (0, 1):
        for step in (1, -1):
            send(h, 0, 0, "all", 1, step)
    store.start()
    total_ref[...] = jnp.zeros_like(total_ref)
    chain[CAP] = jnp.zeros_like(chain[CAP])
    own.wait()
    store.wait()
    multiply(0, 0)
    for step in (1, -1):
        for h in (0, 1):
            a = step % SIDE
            arrived(h, a, 0, "all")
            send(h, a, 0, "lo" if step == 1 else "hi", 0, step)
            for onward in (1, -1):
                send(h, a, 0, "all", 1, onward)
            share(h, a, 0)
    for h in (0, 1):
        arrived(h, 2, 0, "lo")
        arrived(h, 2, 0, "hi")
        for onward in (1, -1):
            send(h, 2, 0, "all", 1, onward)
        share(h, 2, 0)
    turns = iter(TURNS)
    for a in (0, 1, 3, 2):
        for step in (1, -1):
            for h in (0, 1):
                arrived(h, a, step % SIDE, "all")
                send(h, a, step % SIDE, "lo" if step == 1 else "hi", 1, step)
                share(h, a, step % SIDE)
            for chip in next(turns):
                multiply(*chip)
    for a in (0, 1, 3, 2):
        for h in (0, 1):
            for part in ("lo", "hi"):
                arrived(h, a, 2, part)
            share(h, a, 2)
        for chip in next(turns):
            multiply(*chip)
    multiply(2, 2)

    def push(src, dst, send_to, recv_from, peer):
        copy = pltpu.make_async_remote_copy(
            src_ref=src, dst_ref=dst, send_sem=send_to, recv_sem=recv_from, device_id=peer, device_id_type=MESH
        )
        copy.start()
        pending.append(copy)
        return copy

    share_rows = BR_DEV // SIDE
    copies = []
    for step in (2, 1, 3):
        to = lax.rem(y + step, SIDE)
        copies.append(push(
            total_ref.at[pl.ds(to * share_rows, share_rows)], col_buf.at[step - 1], col_send.at[step - 1],
            col_recv.at[step - 1], (lax.axis_index("row"), to),
        ))
    slab = total_ref[pl.ds(y * share_rows, share_rows)]
    for copy in copies:
        copy.wait_recv()
    slab = (slab + (col_buf[0] + col_buf[1] + col_buf[2])).reshape(slab_ref.shape)
    slab_ref[...] = slab
    local_ref[...] = lax.dot_general(
        slab, slab, (((0,), (0,)), ((), ())), precision=HIGHEST, preferred_element_type=jnp.float32
    )

    strip = RANK // 8
    mine = pl.ds(me8 * strip, strip)
    copies = []
    for step in (4, 5, 3, 2, 6, 1, 7):
        peer, number = octet(step)
        copies.append(push(
            local_ref.at[pl.ds(number * strip, strip)], octet_buf.at[step - 1], octet_send.at[step - 1],
            octet_recv.at[step - 1], peer,
        ))
    for copy in copies:
        copy.wait_recv()
    part = local_ref[mine, :] + jnp.sum(octet_buf[...], axis=0)
    me16 = z * SIDE + x
    plane_buf[pl.ds(me16, 1)] = part[None]
    copies = []
    for dz, dx in sorted(((a, b) for a in range(SIDE) for b in range(SIDE) if a + b), key=far, reverse=True):
        s = dz * SIDE + dx - 1
        peer = other(dz, dx)
        copies.append(push(plane_buf.at[me16], plane_buf.at[me16], plane_send.at[s], plane_recv.at[s], peer))
    for copy in copies:
        copy.wait_recv()
    gram_ref[mine, :] = jnp.sum(plane_buf[...], axis=0)
    copies = []
    for step in (4, 5, 3, 2, 6, 1, 7):
        peer, _ = octet(step)
        copies.append(push(
            gram_ref.at[mine], gram_ref.at[mine], last_send.at[step - 1], last_recv.at[step - 1], peer
        ))
    for copy in copies:
        copy.wait_recv()
    for copy in pending:
        copy.wait_send()


def sample(blocks, block_row, block_col, sketch):
    groups = blocks.shape[0] // CAP
    count = sketch.shape[0] // BLK
    dma, f32 = pltpu.SemaphoreType.DMA, jnp.float32
    return pl.pallas_call(
        sampled_kernel,
        out_shape=(
            jax.ShapeDtypeStruct((BR_DEV * BLK // SIDE, RANK), f32),
            jax.ShapeDtypeStruct((RANK, RANK), f32),
        ),
        in_specs=[
            pl.BlockSpec(memory_space=pltpu.SMEM),
            pl.BlockSpec(memory_space=pl.ANY),
            pl.BlockSpec(memory_space=pl.ANY),
        ],
        out_specs=(pl.BlockSpec(memory_space=pltpu.VMEM),) * 2,
        scratch_shapes=[pltpu.VMEM((2, count, BLK, RANK), sketch.dtype)] * (SIDE * SIDE)
        + [
            pltpu.VMEM((groups, CAP, BLK, BLK), blocks.dtype),
            pltpu.VMEM((CAP + 1, BLK, RANK), f32),
            pltpu.VMEM((BR_DEV, BLK, RANK), f32),
            pltpu.VMEM((RANK, RANK), f32),
            pltpu.VMEM((SIDE - 1, BR_DEV // SIDE, BLK, RANK), f32),
            pltpu.VMEM((7, RANK // 8, RANK), f32),
            pltpu.VMEM((SIDE * SIDE, RANK // 8, RANK), f32),
            dma,
            dma,
            dma((48,)),
            dma((48,)),
            dma((32,)),
            dma((32,)),
            dma((3,)),
            dma((3,)),
            dma((7,)),
            dma((7,)),
            dma((15,)),
            dma((15,)),
            dma((7,)),
            dma((7,)),
        ],
        compiler_params=pltpu.CompilerParams(
            collective_id=0, has_side_effects=True, vmem_limit_bytes=53 * 2**20
        ),
    )((block_row << SHIFT) + block_col, blocks.reshape(groups, CAP, BLK, BLK), sketch.reshape(count, BLK, RANK))


def factor_kernel(gram_ref, slab_ref, basis_ref, factor_ref):
    tile = (8, RANK)
    count = RANK // 8
    lane = lax.broadcasted_iota(jnp.int32, tile, 1)
    sub = lax.broadcasted_iota(jnp.int32, tile, 0)
    left = [gram_ref[8 * i : 8 * i + 8, :] for i in range(count)]
    right = [jnp.where(lane == sub + 8 * i, 1.0, 0.0) for i in range(count)]
    inverse = []
    for p in range(count):
        cols = {
            (i, m): jnp.broadcast_to(left[i][:, 8 * p + m : 8 * p + m + 1], tile)
            for i in range(p, count)
            for m in range(8)
        }
        upper = jnp.zeros(tile, jnp.float32)
        lower = jnp.zeros(tile, jnp.float32)
        for k in range(8):
            pivot = jnp.broadcast_to(cols[p, k][k : k + 1, :], tile)
            scale = lax.rsqrt(pivot)
            row = jnp.broadcast_to(left[p][k : k + 1, :], tile) * scale
            inverse_row = jnp.broadcast_to(right[p][k : k + 1, :], tile) * scale
            upper = jnp.where(sub == k, row, upper)
            lower = jnp.where(sub == k, inverse_row, lower)
            ahead = {m: jnp.broadcast_to(cols[p, m][k : k + 1, :], tile) * scale for m in range(k + 1, 8)}
            for i in range(p, count):
                if i == p and k == 7:
                    continue
                weight = cols[i, k] * scale
                for m in range(k + 1, 8):
                    cols[i, m] = cols[i, m] - weight * ahead[m]
                left[i] = left[i] - weight * row
                right[i] = right[i] - weight * inverse_row
        factor_ref[8 * p : 8 * p + 8, :] = jnp.where(lane >= sub + 8 * p, upper, 0.0)
        inverse.append(lower)
    basis_ref[...] = lax.dot_general(
        slab_ref[...],
        jnp.concatenate(inverse, axis=0),
        (((1,), (1,)), ((), ())),
        precision=HIGHEST,
        preferred_element_type=jnp.float32,
    )


def factorise(gram, slab):
    return pl.pallas_call(
        factor_kernel,
        out_shape=(
            jax.ShapeDtypeStruct(slab.shape, jnp.float32),
            jax.ShapeDtypeStruct(gram.shape, jnp.float32),
        ),
        in_specs=[pl.BlockSpec(memory_space=pltpu.VMEM)] * 2,
        out_specs=(pl.BlockSpec(memory_space=pltpu.VMEM),) * 2,
        compiler_params=pltpu.CompilerParams(vmem_limit_bytes=8 * 2**20),
    )(gram, slab)


def shards(blocks, block_row, block_col, sketch):
    slab, gram = sample(blocks, block_row, block_col, sketch)
    return factorise(gram, slab)


def solution(mesh):
    in_specs = (
        P(("row", "col"), None, None),
        P(("row", "col")),
        P(("row", "col")),
        P(("row", "col"), None),
    )
    out_specs = (P(("row", "col"), None), P())
    return jax.shard_map(shards, mesh=mesh, in_specs=in_specs, out_specs=out_specs, check_vma=False)
```

```python
import functools

import jax
import jax.numpy as jnp
from jax import lax
from jax.experimental import pallas as pl
from jax.experimental.pallas import tpu as pltpu
from jax.sharding import PartitionSpec as P

MESH = pl.DeviceIdType.MESH
BLK = 128
RANK = 128
BR_DEV = 8
CAP = 16
SHIFT = 5
SIDE = 4
HIGHEST = lax.Precision.HIGHEST


def place():
    row = lax.axis_index("row")
    return row // 8, lax.rem(row // 2, SIDE), lax.rem(row, 2), lax.axis_index("col")


def row_of(z, x, core):
    return z * 8 + x * 2 + core


def far(step):
    return sum(min(d, SIDE - d) for d in step)


TURNS = (
    (),
    ((0, 1), (1, 0)),
    ((0, 3),),
    ((3, 0),),
    ((1, 1),),
    ((1, 3),),
    ((3, 1),),
    ((3, 3),),
    (),
    ((0, 2), (2, 0), (1, 2), (2, 1)),
    ((3, 2), (2, 3)),
    (),
)


def sampled_kernel(slot_ref, blocks_ref, mine_ref, slab_ref, gram_ref, *scratch):
    held = {(c // SIDE, c % SIDE): scratch[c] for c in range(SIDE * SIDE)}
    stored, chain, total_ref, local_ref, col_buf, octet_buf, plane_buf, *scratch = scratch[SIDE * SIDE :]
    block_sem, own_sem, send_sem, recv_sem, pair_send, pair_recv, *scratch = scratch
    col_send, col_recv, octet_send, octet_recv, plane_send, plane_recv, last_send, last_recv = scratch
    z, x, core, y = place()
    count = mine_ref.shape[0]
    half, quarter = count // 2, count // 4

    barrier = pltpu.get_barrier_semaphore()

    def other(dz, dx):
        return (row_of(lax.rem(z + dz + SIDE, SIDE), lax.rem(x + dx + SIDE, SIDE), core), y)

    me8 = y * 2 + core

    def octet(step):
        number = lax.rem(me8 + step, 8)
        return (row_of(z, x, lax.rem(number, 2)), number // 2), number

    pair = (row_of(z, x, 1 - core), y)
    for peer in (other(0, 1), other(0, -1), other(1, 0), other(-1, 0), *(octet(step)[0] for step in range(1, 8))):
        pl.semaphore_signal(barrier, inc=1, device_id=peer, device_id_type=MESH)
    own = pltpu.make_async_copy(mine_ref, held[0, 0].at[0], own_sem)
    own.start()
    store = pltpu.make_async_copy(blocks_ref, stored, block_sem)
    pl.semaphore_wait(barrier, 11)

    pending = []
    index = {}

    def spot(h, a, b, part, plane):
        start, size = {"all": (h * half, half), "lo": (h * half, quarter), "hi": (h * half + quarter, quarter)}[part]
        return held[(a, b) if h == 0 else (b, a)].at[plane, pl.ds(start, size)]

    def origin(h, a, b, part):
        if (a, b) == (0, 0):
            return mine_ref.at[pl.ds(h * half, half)]
        return spot(h, a, b, part, 0)

    def send(h, a, b, part, axis, step):
        shift = (step, 0) if axis == 0 else (0, step)
        there = (h, (a + shift[0]) % SIDE, (b + shift[1]) % SIDE, part)
        s = index.setdefault(there, len(index))
        copy = pltpu.make_async_remote_copy(
            src_ref=origin(h, a, b, part), dst_ref=spot(*there, 0), send_sem=send_sem.at[s], recv_sem=recv_sem.at[s],
            device_id=other(*(shift[::-1] if h == 0 else shift)), device_id_type=MESH,
        )
        copy.start()
        pending.append(copy)

    def arrived(h, a, b, part):
        s = index[h, a, b, part]
        there = spot(h, a, b, part, 0)
        pltpu.make_async_remote_copy(
            src_ref=there, dst_ref=there, send_sem=send_sem.at[s], recv_sem=recv_sem.at[s], device_id=pair,
            device_id_type=MESH,
        ).wait_recv()

    shared = {}

    def share(h, a, b):
        s = len(shared)
        copy = pltpu.make_async_remote_copy(
            src_ref=origin(h, a, b, "all"), dst_ref=spot(h, a, b, "all", 1), send_sem=pair_send.at[s],
            recv_sem=pair_recv.at[s], device_id=pair, device_id_type=MESH,
        )
        copy.start()
        pending.append(copy)
        shared[h, a, b] = copy

    def multiply(dx, dz):
        shared[0, dx, dz].wait_recv()
        shared[1, dz, dx].wait_recv()
        sketch = held[dx, dz]

        def one_group(plane, _):
            group = row_of(lax.rem(z - dz + SIDE, SIDE), lax.rem(x - dx + SIDE, SIDE), lax.rem(core + plane, 2))
            last = [CAP] * BR_DEV
            for k in range(CAP):
                code = slot_ref[group * CAP + k]
                row, col = code >> SHIFT, code & (2**SHIFT - 1)
                before = CAP
                for b in range(BR_DEV):
                    same = row == b
                    before = jnp.where(same, last[b], before)
                    last[b] = jnp.where(same, k, last[b])
                product = jnp.dot(stored[group, k], sketch[plane, col], preferred_element_type=jnp.float32)
                chain[k] = product + chain[before]
            for b in range(BR_DEV):
                total_ref[b] += chain[last[b]]
            return 0

        lax.fori_loop(0, 2, one_group, 0)

    for h in (0, 1):
        for step in (1, -1):
            send(h, 0, 0, "all", 0, step)
    for h in (0, 1):
        share(h, 0, 0)
    for h in (0, 1):
        for step in (1, -1):
            send(h, 0, 0, "all", 1, step)
    store.start()
    total_ref[...] = jnp.zeros_like(total_ref)
    chain[CAP] = jnp.zeros_like(chain[CAP])
    own.wait()
    store.wait()
    multiply(0, 0)
    for step in (1, -1):
        for h in (0, 1):
            a = step % SIDE
            arrived(h, a, 0, "all")
            send(h, a, 0, "lo" if step == 1 else "hi", 0, step)
            for onward in (1, -1):
                send(h, a, 0, "all", 1, onward)
            share(h, a, 0)
    for h in (0, 1):
        arrived(h, 2, 0, "lo")
        arrived(h, 2, 0, "hi")
        for onward in (1, -1):
            send(h, 2, 0, "all", 1, onward)
        share(h, 2, 0)
    turns = iter(TURNS)
    for a in (0, 1, 3, 2):
        for step in (1, -1):
            for h in (0, 1):
                arrived(h, a, step % SIDE, "all")
                send(h, a, step % SIDE, "lo" if step == 1 else "hi", 1, step)
                share(h, a, step % SIDE)
            for chip in next(turns):
                multiply(*chip)
    for a in (0, 1, 3, 2):
        for h in (0, 1):
            for part in ("lo", "hi"):
                arrived(h, a, 2, part)
            share(h, a, 2)
        for chip in next(turns):
            multiply(*chip)
    multiply(2, 2)

    def push(src, dst, send_to, recv_from, peer):
        copy = pltpu.make_async_remote_copy(
            src_ref=src, dst_ref=dst, send_sem=send_to, recv_sem=recv_from, device_id=peer, device_id_type=MESH
        )
        copy.start()
        pending.append(copy)
        return copy

    share_rows = BR_DEV // SIDE
    copies = []
    for step in (2, 1, 3):
        to = lax.rem(y + step, SIDE)
        copies.append(push(
            total_ref.at[pl.ds(to * share_rows, share_rows)], col_buf.at[step - 1], col_send.at[step - 1],
            col_recv.at[step - 1], (lax.axis_index("row"), to),
        ))
    slab = total_ref[pl.ds(y * share_rows, share_rows)]
    for copy in copies:
        copy.wait_recv()
    slab = (slab + (col_buf[0] + col_buf[1] + col_buf[2])).reshape(slab_ref.shape)
    slab_ref[...] = slab
    local_ref[...] = lax.dot_general(
        slab, slab, (((0,), (0,)), ((), ())), precision=HIGHEST, preferred_element_type=jnp.float32
    )

    strip = RANK // 8
    mine = pl.ds(me8 * strip, strip)
    copies = []
    for step in (4, 5, 3, 2, 6, 1, 7):
        peer, number = octet(step)
        copies.append(push(
            local_ref.at[pl.ds(number * strip, strip)], octet_buf.at[step - 1], octet_send.at[step - 1],
            octet_recv.at[step - 1], peer,
        ))
    for copy in copies:
        copy.wait_recv()
    part = local_ref[mine, :] + jnp.sum(octet_buf[...], axis=0)
    me16 = z * SIDE + x
    plane_buf[pl.ds(me16, 1)] = part[None]
    copies = []
    for dz, dx in sorted(((a, b) for a in range(SIDE) for b in range(SIDE) if a + b), key=far, reverse=True):
        s = dz * SIDE + dx - 1
        peer = other(dz, dx)
        copies.append(push(plane_buf.at[me16], plane_buf.at[me16], plane_send.at[s], plane_recv.at[s], peer))
    for copy in copies:
        copy.wait_recv()
    gram_ref[mine, :] = jnp.sum(plane_buf[...], axis=0)
    copies = []
    for step in (4, 5, 3, 2, 6, 1, 7):
        peer, _ = octet(step)
        copies.append(push(
            gram_ref.at[mine], gram_ref.at[mine], last_send.at[step - 1], last_recv.at[step - 1], peer
        ))
    for copy in copies:
        copy.wait_recv()
    for copy in pending:
        copy.wait_send()


def sample(blocks, block_row, block_col, sketch):
    groups = blocks.shape[0] // CAP
    count = sketch.shape[0] // BLK
    dma, f32 = pltpu.SemaphoreType.DMA, jnp.float32
    return pl.pallas_call(
        sampled_kernel,
        out_shape=(
            jax.ShapeDtypeStruct((BR_DEV * BLK // SIDE, RANK), f32),
            jax.ShapeDtypeStruct((RANK, RANK), f32),
        ),
        in_specs=[
            pl.BlockSpec(memory_space=pltpu.SMEM),
            pl.BlockSpec(memory_space=pl.ANY),
            pl.BlockSpec(memory_space=pl.ANY),
        ],
        out_specs=(pl.BlockSpec(memory_space=pltpu.VMEM),) * 2,
        scratch_shapes=[pltpu.VMEM((2, count, BLK, RANK), sketch.dtype)] * (SIDE * SIDE)
        + [
            pltpu.VMEM((groups, CAP, BLK, BLK), blocks.dtype),
            pltpu.VMEM((CAP + 1, BLK, RANK), f32),
            pltpu.VMEM((BR_DEV, BLK, RANK), f32),
            pltpu.VMEM((RANK, RANK), f32),
            pltpu.VMEM((SIDE - 1, BR_DEV // SIDE, BLK, RANK), f32),
            pltpu.VMEM((7, RANK // 8, RANK), f32),
            pltpu.VMEM((SIDE * SIDE, RANK // 8, RANK), f32),
            dma,
            dma,
            dma((48,)),
            dma((48,)),
            dma((32,)),
            dma((32,)),
            dma((3,)),
            dma((3,)),
            dma((7,)),
            dma((7,)),
            dma((15,)),
            dma((15,)),
            dma((7,)),
            dma((7,)),
        ],
        compiler_params=pltpu.CompilerParams(
            collective_id=0, has_side_effects=True, vmem_limit_bytes=53 * 2**20
        ),
    )((block_row << SHIFT) + block_col, blocks.reshape(groups, CAP, BLK, BLK), sketch.reshape(count, BLK, RANK))


def factor_kernel(gram_ref, slab_ref, basis_ref, factor_ref):
    tile = (8, RANK)
    count = RANK // 8
    lane = lax.broadcasted_iota(jnp.int32, tile, 1)
    sub = lax.broadcasted_iota(jnp.int32, tile, 0)
    left = [gram_ref[8 * i : 8 * i + 8, :] for i in range(count)]
    right = [jnp.where(lane == sub + 8 * i, 1.0, 0.0) for i in range(count)]
    inverse = []
    for p in range(count):
        cols = {
            (i, m): jnp.broadcast_to(left[i][:, 8 * p + m : 8 * p + m + 1], tile)
            for i in range(p, count)
            for m in range(8)
        }
        upper = jnp.zeros(tile, jnp.float32)
        lower = jnp.zeros(tile, jnp.float32)
        for k in range(8):
            pivot = jnp.broadcast_to(cols[p, k][k : k + 1, :], tile)
            scale = lax.rsqrt(pivot)
            row = jnp.broadcast_to(left[p][k : k + 1, :], tile) * scale
            inverse_row = jnp.broadcast_to(right[p][k : k + 1, :], tile) * scale
            upper = jnp.where(sub == k, row, upper)
            lower = jnp.where(sub == k, inverse_row, lower)
            ahead = {m: jnp.broadcast_to(cols[p, m][k : k + 1, :], tile) * scale for m in range(k + 1, 8)}
            for i in range(p, count):
                if i == p and k == 7:
                    continue
                weight = cols[i, k] * scale
                for m in range(k + 1, 8):
                    cols[i, m] = cols[i, m] - weight * ahead[m]
                left[i] = left[i] - weight * row
                right[i] = right[i] - weight * inverse_row
        factor_ref[8 * p : 8 * p + 8, :] = jnp.where(lane >= sub + 8 * p, upper, 0.0)
        inverse.append(lower)
    basis_ref[...] = lax.dot_general(
        slab_ref[...],
        jnp.concatenate(inverse, axis=0),
        (((1,), (1,)), ((), ())),
        precision=HIGHEST,
        preferred_element_type=jnp.float32,
    )


def factorise(gram, slab):
    return pl.pallas_call(
        factor_kernel,
        out_shape=(
            jax.ShapeDtypeStruct(slab.shape, jnp.float32),
            jax.ShapeDtypeStruct(gram.shape, jnp.float32),
        ),
        in_specs=[pl.BlockSpec(memory_space=pltpu.VMEM)] * 2,
        out_specs=(pl.BlockSpec(memory_space=pltpu.VMEM),) * 2,
        compiler_params=pltpu.CompilerParams(vmem_limit_bytes=8 * 2**20),
    )(gram, slab)


def shards(blocks, block_row, block_col, sketch):
    slab, gram = sample(blocks, block_row, block_col, sketch)
    return factorise(gram, slab)


def solution(mesh):
    in_specs = (
        P(("row", "col"), None, None),
        P(("row", "col")),
        P(("row", "col")),
        P(("row", "col"), None),
    )
    out_specs = (P(("row", "col"), None), P())
    return jax.shard_map(shards, mesh=mesh, in_specs=in_specs, out_specs=out_specs, check_vma=False)
```
